32 devices in a mesh: dp: 8 (over y, x, core), seq: 4 (over z).
Axes of the slice: x: 2, y: 2, z: 4, core: 2. Of those that a mesh axis runs over, the one named last changes fastest.
Arguments:
- tokens: bfloat16 [8, 1024, 896], P('dp', 'seq'), may hold values from -6 to 6
- segments: int32 [8, 1024], P('dp', 'seq'), may hold values from 0 to 2, as said below
- cotangent: bfloat16 [8, 1024, 896], P('dp', 'seq'), may hold values from -6 to 6
- attn_gain: bfloat16 [896], P('seq'), may hold values from 0.5 to 1.5
- w_query: bfloat16 [896, 896], P('dp', 'seq'), may hold values from -0.1875 to 0.1875
- b_query: bfloat16 [896], P('seq'), may hold values from -3 to 3
- w_key: bfloat16 [896, 128], P('dp', 'seq'), may hold values from -0.1875 to 0.1875
- b_key: bfloat16 [128], P('seq'), may hold values from -3 to 3
- w_value: bfloat16 [896, 128], P('dp', 'seq'), may hold values from -0.1875 to 0.1875
- b_value: bfloat16 [128], P('seq'), may hold values from -3 to 3
- w_out: bfloat16 [896, 896], P('dp', 'seq'), may hold values from -0.75 to 0.75
- mlp_gain: bfloat16 [896], P('seq'), may hold values from 0.5 to 1.5
- w_gate: bfloat16 [896, 4864], P('dp', 'seq'), may hold values from -0.1875 to 0.1875
- w_up: bfloat16 [896, 4864], P('dp', 'seq'), may hold values from -0.1875 to 0.1875
- w_down: bfloat16 [4864, 896], P('seq', 'dp'), may hold values from -0.078125 to 0.078125
Outputs:
- output: bfloat16 [8, 1024, 896], P('dp', 'seq')
- input_grad: float32 [8, 1024, 896], P('dp', 'seq')
- grad_attn_gain: float32 [896], P('seq')
- grad_w_query: float32 [896, 896], P('dp', 'seq')
- grad_b_query: float32 [896], P('seq')
- grad_w_key: float32 [896, 128], P('dp', 'seq')
- grad_b_key: float32 [128], P('seq')
- grad_w_value: float32 [896, 128], P('dp', 'seq')
- grad_b_value: float32 [128], P('seq')
- grad_w_out: float32 [896, 896], P('dp', 'seq')
- grad_mlp_gain: float32 [896], P('seq')
- grad_w_gate: float32 [896, 4864], P('dp', 'seq')
- grad_w_up: float32 [896, 4864], P('dp', 'seq')
- grad_w_down: float32 [4864, 896], P('seq', 'dp')
The draws below stay inside these ranges and needn't reach their ends.
Inputs may be any that keep to these rules, and one draw needn't show every extreme that they name: `segments`: in each sequence the numbers start at 0 and never fall; document 1 begins within the first 256 tokens and ends within the last 256.
All inputs are finite; a program needn't handle non-finite values.
Results may differ from the reference program's by a relative error of at most 0.02.
Values may be sent and summed in bfloat16 or wider, within the bound.
A program may use at most 192 MiB of HBM per device.

```python
import jax
import jax.numpy as jnp
from jax import lax

D = 896
H = 14
KVH = 2
HD = 64
FF = 4864
LEN = 1024
MICRO = 2
KVW = 128
SEQS = 8
N_SEQ = 4


def draw_segments(key, part):
    key = jax.random.fold_in(key, 11)
    start_key, end_key = jax.random.split(key)
    block_len = LEN // N_SEQ
    starts = jax.random.randint(start_key, (SEQS, 1), 1, block_len)
    ends = jax.random.randint(end_key, (SEQS, 1), LEN - block_len + 1, LEN)
    places = jnp.arange(LEN)[None, :]
    seg_ids = (places >= starts).astype(jnp.int32) + (places >= ends).astype(jnp.int32)
    return seg_ids.astype(jnp.int32)


def shard_levels(own_key, extent, shards, low, top_value):
    level, own = 1.0, jax.random.fold_in(own_key, 6)
    for dim, blocks in shards:
        heights = jnp.exp(jax.random.uniform(jax.random.fold_in(own, dim), (blocks,), jnp.float32, low / len(shards), top_value / len(shards)))
        level = level * jnp.repeat(heights, extent[dim] // blocks).reshape([-1 if axis == dim else 1 for axis in range(len(extent))])
    return level


def scatter_about(key, shape, spread, reach, cuts=(), kind=jnp.bfloat16):
    values = jax.random.normal(key, shape, jnp.float32) * spread
    if len(cuts) > 0:
        values = shard_levels(key, shape, cuts, -0.22, 0.18) * values
    return jnp.clip(values, min=-reach, max=reach).astype(kind)


def setup_inputs(seed: int = 0) -> dict:
    keys = jax.random.split(jax.random.key(seed), 16)
    tokens = scatter_about(keys[0], (SEQS, LEN, D), 1.0, 6.0, ((0, 8), (1, 4)))
    segments = draw_segments(jax.random.fold_in(keys[15], 71), 0)
    cotangent = scatter_about(keys[2], (SEQS, LEN, D), 1.0, 6.0, ((0, 8), (1, 4)))
    attn_gain = jnp.clip(1.0 + 0.1 * jax.random.normal(keys[3], (D,), jnp.float32), 0.5, 1.5).astype(jnp.bfloat16)
    w_query = scatter_about(keys[4], (D, D), D ** -0.5, 0.1875, ((0, 8), (1, 4)))
    b_query = scatter_about(keys[5], (D,), 0.5, 3.0, ((0, 4),))
    w_key = scatter_about(keys[6], (D, KVW), D ** -0.5, 0.1875, ((0, 8), (1, 4)))
    b_key = scatter_about(keys[7], (KVW,), 0.5, 3.0, ((0, 4),))
    w_value = scatter_about(keys[8], (D, KVW), D ** -0.5, 0.1875, ((0, 8), (1, 4)))
    b_value = scatter_about(keys[9], (KVW,), 0.5, 3.0, ((0, 4),))
    w_out = scatter_about(keys[10], (D, D), (D // 16) ** -0.5, 0.75, ((0, 8), (1, 4)))
    mlp_gain = jnp.clip(1.0 + 0.1 * jax.random.normal(keys[11], (D,), jnp.float32), 0.5, 1.5).astype(jnp.bfloat16)
    w_gate = scatter_about(keys[12], (D, FF), D ** -0.5, 0.1875, ((0, 8), (1, 4)))
    w_up = scatter_about(keys[13], (D, FF), D ** -0.5, 0.1875, ((0, 8), (1, 4)))
    w_down = scatter_about(keys[14], (FF, D), FF ** -0.5, 0.078125, ((0, 4), (1, 8)))
    return {"tokens": tokens, "segments": segments, "cotangent": cotangent, "attn_gain": attn_gain, "w_query": w_query, "b_query": b_query, "w_key": w_key, "b_key": b_key, "w_value": w_value, "b_value": b_value, "w_out": w_out, "mlp_gain": mlp_gain, "w_gate": w_gate, "w_up": w_up, "w_down": w_down}


@jax.custom_vjp
def low(v):
    return lax.optimization_barrier(v.astype(jnp.bfloat16)).astype(jnp.float32)

@jax.custom_vjp
def low_back(v):
    return v

def low_keep(v):
    return (low(v), None)

def low_pass(kept, grad):
    return (grad,)

def back_keep(v):
    return (v, None)

def back_low(kept, grad):
    return (low(grad),)
low.defvjp(low_keep, low_pass)
low_back.defvjp(back_keep, back_low)
norm_eps = 1e-06
rope_base = 1000000.0
exact_mode = lax.Precision.HIGHEST

def product(left_mat, right_mat):
    return jnp.dot(left_mat, right_mat, precision=exact_mode, preferred_element_type=jnp.float32)

def rotate(heads_field, positions):
    half_dim = heads_field.shape[-1] // 2
    frequency = rope_base ** (-2.0 * jnp.arange(half_dim, dtype=jnp.float32) / heads_field.shape[-1])
    angles = positions.astype(jnp.float32)[:, None] * frequency[None, :]
    cosine = jnp.cos(angles)[:, None, :]
    sine_table = jnp.sin(angles)[:, None, :]
    first_half = heads_field[..., :half_dim]
    second = heads_field[..., half_dim:]
    return jnp.concatenate([first_half * cosine - second * sine_table, second * cosine + first_half * sine_table], axis=-1)

def layer(tokens, seg_ids, attn_gain, w_query, b_query, w_key, b_key, w_value, b_value, w_out, mlp_gain, w_gate, w_up, w_down):
    group_count, length, model_width = tokens.shape
    flat_rows = tokens.reshape(group_count * length, model_width)
    scale_one = lax.rsqrt(lax.optimization_barrier(jnp.mean(flat_rows * flat_rows, axis=-1, keepdims=True)) + norm_eps)
    normed = low(flat_rows * scale_one * attn_gain)
    query_lin = low_back(product(normed, w_query) + b_query)
    key_lin = low_back(product(normed, w_key) + b_key)
    value_lin = low_back(product(normed, w_value) + b_value)
    places = jnp.arange(length)
    query_rot = low(rotate(query_lin.reshape(group_count, length, H, HD), places))
    key_rot = low(rotate(key_lin.reshape(group_count, length, KVH, HD), places))
    values = low(value_lin.reshape(group_count, length, KVH, HD))
    query_rot = query_rot.reshape(group_count, length, KVH, H // KVH, HD)
    scores = low_back(jnp.einsum('bqgjd,bkgd->bgjqk', query_rot, key_rot, precision=exact_mode) * 0.125)
    allowed = (seg_ids[:, :, None] == seg_ids[:, None, :]) & (places[:, None] >= places[None, :])
    masked = jnp.where(allowed[:, None, None], scores, -1e+30)
    highest = lax.optimization_barrier(jnp.max(masked, axis=-1, keepdims=True))
    weights = jnp.exp(masked - highest)
    prob_low = low(weights / lax.optimization_barrier(jnp.sum(weights, axis=-1, keepdims=True)))
    attended = jnp.einsum('bgjqk,bkgd->bqgjd', prob_low, values, precision=exact_mode)
    mixed_heads = low(low_back(attended.reshape(group_count * length, model_width)))
    residual = flat_rows + low_back(product(mixed_heads, w_out))
    scale_two = lax.rsqrt(lax.optimization_barrier(jnp.mean(residual * residual, axis=-1, keepdims=True)) + norm_eps)
    normed_two = low(residual * scale_two * mlp_gain)
    gate_lin = low_back(product(normed_two, w_gate))
    up_lin = low_back(product(normed_two, w_up))
    hidden = low(gate_lin / (1.0 + jnp.exp(-gate_lin)) * up_lin)
    result = residual + low_back(product(hidden, w_down))
    return result.reshape(group_count, length, model_width)

def reference(tokens, segments, cotangent, attn_gain, w_query, b_query, w_key, b_key, w_value, b_value, w_out, mlp_gain, w_gate, w_up, w_down):
    params = tuple((weight_item.astype(jnp.float32) for weight_item in (attn_gain, w_query, b_query, w_key, b_key, w_value, b_value, w_out, mlp_gain, w_gate, w_up, w_down)))
    blocks = tokens.astype(jnp.float32).reshape(SEQS // MICRO, MICRO, LEN, D)
    seg_blocks = segments.reshape(SEQS // MICRO, MICRO, LEN)
    cot_blocks = cotangent.astype(jnp.float32).reshape(SEQS // MICRO, MICRO, LEN, D)

    def step_block(running, item_block):
        token_block, seg_block, cot_block = item_block

        def forward(inputs, *weight_list):
            return layer(inputs, seg_block, *weight_list)
        output, pullback = jax.vjp(forward, token_block, *params)
        gradients = pullback(cot_block)
        running = tuple((total_item + grad_item for total_item, grad_item in zip(running, gradients[1:])))
        return (running, (output.astype(jnp.bfloat16), gradients[0]))
    zeros_init = tuple((jnp.zeros(weight_item.shape, jnp.float32) for weight_item in params))
    grad_sums, (outputs, input_grads) = lax.scan(step_block, zeros_init, (blocks, seg_blocks, cot_blocks))
    return (outputs.reshape(SEQS, LEN, D), input_grads.reshape(SEQS, LEN, D), grad_sums[0], grad_sums[1], grad_sums[2], grad_sums[3], grad_sums[4], grad_sums[5], grad_sums[6], grad_sums[7], grad_sums[8], grad_sums[9], grad_sums[10], grad_sums[11])
```

```python
import jax
import jax.numpy as jnp
from jax import lax
from jax.sharding import PartitionSpec as P

H = 14
KVH = 2
HD = 64


norm_eps = 1e-06
rope_base = 1000000.0


def contract(left_mat, right_mat, left_dim, right_dim):
    return lax.dot_general(
        left_mat,
        right_mat,
        (((left_dim,), (right_dim,)), ((), ())),
        preferred_element_type=jnp.float32,
    )


def angle_tables(positions, head_dim):
    half_dim = head_dim // 2
    frequency = rope_base ** (-2.0 * jnp.arange(half_dim, dtype=jnp.float32) / head_dim)
    angles = positions.astype(jnp.float32)[:, None] * frequency[None, :]
    return (jnp.cos(angles)[:, None, :], jnp.sin(angles)[:, None, :])


def rotate(heads_field, cosine, sine_table):
    half_dim = heads_field.shape[-1] // 2
    first_half = heads_field[..., :half_dim]
    second = heads_field[..., half_dim:]
    return jnp.concatenate(
        [first_half * cosine - second * sine_table, second * cosine + first_half * sine_table],
        axis=-1,
    )


def unrotate(grad_field, cosine, sine_table):
    half_dim = grad_field.shape[-1] // 2
    first_half = grad_field[..., :half_dim]
    second = grad_field[..., half_dim:]
    return jnp.concatenate(
        [first_half * cosine + second * sine_table, second * cosine - first_half * sine_table],
        axis=-1,
    )


def score_block(query_rot, key_all, query_seg, key_seg, query_pos, key_pos):
    scores = (
        jnp.einsum("qgjd,kgd->gjqk", query_rot, key_all, preferred_element_type=jnp.float32) * 0.125
    )
    allowed = (query_seg[:, None] == key_seg[None, :]) & (query_pos[:, None] >= key_pos[None, :])
    return jnp.where(allowed, scores, -1e30)


def on_device(
    tokens,
    segments,
    cotangent,
    attn_gain,
    w_query,
    b_query,
    w_key,
    b_key,
    w_value,
    b_value,
    w_out,
    mlp_gain,
    w_gate,
    w_up,
    w_down,
):
    local_len = tokens.shape[1]
    model_width = tokens.shape[2]
    seq_count = lax.axis_size("seq")
    dp_count = lax.axis_size("dp")
    seq_place = lax.axis_index("seq")
    full_len = local_len * seq_count
    group_size = H // KVH
    kv_width = KVH * HD
    rows = w_query.shape[0]
    q_cols = w_query.shape[1]
    k_cols = w_key.shape[1]
    pack_cols = 2 * q_cols + 2 * k_cols

    def as_row(vector):
        return jnp.pad(vector, (0, pack_cols - vector.shape[0]))[None]

    packed = jnp.concatenate(
        [
            jnp.concatenate([w_query, w_out, w_key, w_value], axis=1),
            jnp.concatenate([attn_gain, b_query, b_key, b_value])[None],
            as_row(mlp_gain),
            as_row(segments[0].astype(jnp.bfloat16)),
            jnp.zeros((13, pack_cols), jnp.bfloat16),
        ],
        axis=0,
    )
    by_seq = lax.all_gather(packed, "seq", axis=0)
    attn_all = lax.all_gather(by_seq[:, :rows], "dp", axis=0)
    attn_all = attn_all.transpose(0, 2, 1, 3).reshape(model_width, seq_count, pack_cols)
    mat_query = attn_all[:, :, :q_cols].reshape(model_width, model_width)
    mat_out = attn_all[:, :, q_cols : 2 * q_cols].reshape(model_width, model_width)
    mat_key = attn_all[:, :, 2 * q_cols : 2 * q_cols + k_cols].reshape(model_width, kv_width)
    mat_value = attn_all[:, :, 2 * q_cols + k_cols :].reshape(model_width, kv_width)
    vectors = by_seq[:, rows].astype(jnp.float32)
    gain_one = vectors[:, :q_cols].reshape(model_width)
    bias_query = vectors[:, q_cols : 2 * q_cols].reshape(model_width)
    bias_key = vectors[:, 2 * q_cols : 2 * q_cols + k_cols].reshape(kv_width)
    bias_value = vectors[:, 2 * q_cols + k_cols :].reshape(kv_width)
    gain_two = by_seq[:, rows + 1, :q_cols].astype(jnp.float32).reshape(model_width)
    seg_all = by_seq[:, rows + 2, :local_len].reshape(full_len)
    seg_own = segments[0].astype(jnp.bfloat16)

    mat_gate = lax.all_gather(w_gate, "dp", axis=0, tiled=True)
    mat_up = lax.all_gather(w_up, "dp", axis=0, tiled=True)
    mat_down = lax.all_gather(w_down.T, "dp", axis=0, tiled=True)
    d_result = cotangent[0]
    d_result_all = lax.all_gather(d_result, "seq", axis=0, tiled=True)

    own_pos = seq_place * local_len + jnp.arange(local_len, dtype=jnp.int32)
    all_pos = jnp.arange(full_len, dtype=jnp.int32)
    cosine, sine_table = angle_tables(own_pos, HD)
    inputs = tokens[0].astype(jnp.float32)
    scale_one = lax.rsqrt(jnp.mean(inputs * inputs, axis=-1, keepdims=True) + norm_eps)
    normed = (inputs * scale_one * gain_one).astype(jnp.bfloat16)
    query_lin = jnp.dot(normed, mat_query, preferred_element_type=jnp.float32) + bias_query
    key_lin = jnp.dot(normed, mat_key, preferred_element_type=jnp.float32) + bias_key
    value_lin = jnp.dot(normed, mat_value, preferred_element_type=jnp.float32) + bias_value
    query_rot = rotate(query_lin.reshape(local_len, H, HD), cosine, sine_table).astype(
        jnp.bfloat16
    )
    query_rot = query_rot.reshape(local_len, KVH, group_size, HD)
    key_rot = rotate(key_lin.reshape(local_len, KVH, HD), cosine, sine_table).astype(jnp.bfloat16)
    value_loc = value_lin.astype(jnp.bfloat16)
    kv_loc = jnp.concatenate([key_rot.reshape(local_len, kv_width), value_loc], axis=1)
    kv_all = lax.all_gather(kv_loc, "seq", axis=0, tiled=True)
    key_all = kv_all[:, :kv_width].reshape(full_len, KVH, HD)
    value_all = kv_all[:, kv_width:].reshape(full_len, KVH, HD)
    masked = score_block(query_rot, key_all, seg_own, seg_all, own_pos, all_pos)
    highest = jnp.max(masked, axis=-1, keepdims=True)
    weights = jnp.exp(masked - highest)
    totals = jnp.sum(weights, axis=-1, keepdims=True)
    prob_low = (weights / totals).astype(jnp.bfloat16)
    log_total = highest + jnp.log(totals)
    mixed = jnp.einsum("gjqk,kgd->qgjd", prob_low, value_all, preferred_element_type=jnp.float32)
    mixed = mixed.astype(jnp.bfloat16).reshape(local_len, model_width)
    residual = inputs + jnp.dot(mixed, mat_out, preferred_element_type=jnp.float32)
    scale_two = lax.rsqrt(jnp.mean(residual * residual, axis=-1, keepdims=True) + norm_eps)
    normed_loc = (residual * scale_two * gain_two).astype(jnp.bfloat16)

    normed_two = lax.all_gather(normed_loc, "seq", axis=0, tiled=True)
    gate_lin = jnp.dot(normed_two, mat_gate, preferred_element_type=jnp.float32)
    up_lin = jnp.dot(normed_two, mat_up, preferred_element_type=jnp.float32)
    d_hidden = jnp.dot(d_result_all, mat_down, preferred_element_type=jnp.float32)
    sigmoid_gate = 1.0 / (1.0 + jnp.exp(-gate_lin))
    silu_gate = gate_lin * sigmoid_gate
    hidden = (silu_gate * up_lin).astype(jnp.bfloat16)
    d_gate = (
        d_hidden * up_lin * (sigmoid_gate + gate_lin * sigmoid_gate * (1.0 - sigmoid_gate))
    ).astype(jnp.bfloat16)
    d_up = (d_hidden * silu_gate).astype(jnp.bfloat16)
    d_norm_all = (contract(d_gate, mat_gate, 1, 1) + contract(d_up, mat_up, 1, 1)).astype(
        jnp.bfloat16
    )
    d_norm_part = lax.psum_scatter(d_norm_all, "seq", scatter_dimension=0, tiled=True).astype(
        jnp.float32
    )
    branch_all = contract(hidden, mat_down, 1, 1).astype(jnp.bfloat16)
    branch_sum = lax.psum_scatter(branch_all, "seq", scatter_dimension=0, tiled=True)
    output = (residual + branch_sum.astype(jnp.float32)).astype(jnp.bfloat16)[None]
    grad_gate, grad_up, grad_down = (
        lax.psum_scatter(
            contract(left, right, 0, 0).astype(jnp.bfloat16), "dp", scatter_dimension=0, tiled=True
        ).astype(jnp.float32)
        for left, right in ((normed_two, d_gate), (normed_two, d_up), (d_result_all, hidden))
    )

    grad_gain_two = jnp.sum(d_norm_part * residual * scale_two, axis=0)
    d_scaled_two = d_norm_part * gain_two
    d_residual = (
        d_result.astype(jnp.float32)
        + scale_two * d_scaled_two
        - residual * scale_two**3 * jnp.mean(d_scaled_two * residual, axis=-1, keepdims=True)
    )
    d_attn = d_residual.astype(jnp.bfloat16)
    grad_out = contract(mixed, d_attn, 0, 0)
    d_mixed = (
        contract(d_attn, mat_out, 1, 1)
        .astype(jnp.bfloat16)
        .reshape(local_len, KVH, group_size, HD)
    )
    masked = score_block(query_rot, key_all, seg_own, seg_all, own_pos, all_pos)
    prob_full = jnp.exp(masked - log_total)
    prob_low = prob_full.astype(jnp.bfloat16)
    d_probs = jnp.einsum("qgjd,kgd->gjqk", d_mixed, value_all, preferred_element_type=jnp.float32)
    d_value_full = jnp.einsum(
        "gjqk,qgjd->kgd", prob_low, d_mixed, preferred_element_type=jnp.float32
    )
    d_scores = (
        prob_full * (d_probs - jnp.sum(d_probs * prob_full, axis=-1, keepdims=True))
    ).astype(jnp.bfloat16)
    d_key_full = (
        jnp.einsum("gjqk,qgjd->kgd", d_scores, query_rot, preferred_element_type=jnp.float32)
        * 0.125
    )
    d_kv_full = jnp.concatenate(
        [d_key_full.reshape(full_len, kv_width), d_value_full.reshape(full_len, kv_width)], axis=1
    ).astype(jnp.bfloat16)
    d_kv_loc = lax.psum_scatter(d_kv_full, "seq", scatter_dimension=0, tiled=True)
    d_query_rot = (
        jnp.einsum("gjqk,kgd->qgjd", d_scores, key_all, preferred_element_type=jnp.float32) * 0.125
    ).reshape(local_len, H, HD)
    d_query_lin = (
        unrotate(d_query_rot, cosine, sine_table)
        .astype(jnp.bfloat16)
        .reshape(local_len, model_width)
    )
    d_key_loc = d_kv_loc[:, :kv_width].astype(jnp.float32).reshape(local_len, KVH, HD)
    d_key_lin = (
        unrotate(d_key_loc, cosine, sine_table).astype(jnp.bfloat16).reshape(local_len, kv_width)
    )
    d_value_lin = d_kv_loc[:, kv_width:]
    grad_query = contract(normed, d_query_lin, 0, 0)
    grad_key = contract(normed, d_key_lin, 0, 0)
    grad_value = contract(normed, d_value_lin, 0, 0)

    attn_grads = jnp.concatenate(
        [
            item.astype(jnp.bfloat16).reshape(dp_count, rows, seq_count, -1)
            for item in (grad_query, grad_out, grad_key, grad_value)
        ],
        axis=3,
    ).transpose(0, 2, 1, 3)
    attn_grads = lax.psum_scatter(attn_grads, "dp", scatter_dimension=0)
    attn_grads = lax.psum_scatter(attn_grads, "seq", scatter_dimension=0).astype(jnp.float32)

    grad_bias_query = jnp.sum(d_query_lin, axis=0, dtype=jnp.float32)
    grad_bias_key = jnp.sum(d_key_lin, axis=0, dtype=jnp.float32)
    grad_bias_value = jnp.sum(d_value_lin, axis=0, dtype=jnp.float32)
    d_normed = (
        contract(d_query_lin, mat_query, 1, 1)
        + contract(d_key_lin, mat_key, 1, 1)
        + contract(d_value_lin, mat_value, 1, 1)
    )
    grad_gain_one = jnp.sum(d_normed * inputs * scale_one, axis=0)
    d_scaled = d_normed * gain_one
    d_inputs = (
        d_residual
        + scale_one * d_scaled
        - inputs * scale_one**3 * jnp.mean(d_scaled * inputs, axis=-1, keepdims=True)
    )
    small = jnp.concatenate(
        [
            item.reshape(seq_count, -1)
            for item in (
                grad_gain_one,
                grad_bias_query,
                grad_gain_two,
                grad_bias_key,
                grad_bias_value,
            )
        ],
        axis=1,
    )
    small = lax.psum(small, ("dp", "seq"))
    small = lax.dynamic_index_in_dim(small, seq_place, 0, keepdims=False)
    return (
        output,
        d_inputs[None],
        small[:q_cols],
        attn_grads[:, :q_cols],
        small[q_cols : 2 * q_cols],
        attn_grads[:, 2 * q_cols : 2 * q_cols + k_cols],
        small[3 * q_cols : 3 * q_cols + k_cols],
        attn_grads[:, 2 * q_cols + k_cols :],
        small[3 * q_cols + k_cols :],
        attn_grads[:, q_cols : 2 * q_cols],
        small[2 * q_cols : 3 * q_cols],
        grad_gate,
        grad_up,
        grad_down.T,
    )


def solution(mesh):
    return jax.shard_map(
        on_device,
        mesh=mesh,
        in_specs=(
            P("dp", "seq", None),
            P("dp", "seq"),
            P("dp", "seq", None),
            P("seq"),
            P("dp", "seq"),
            P("seq"),
            P("dp", "seq"),
            P("seq"),
            P("dp", "seq"),
            P("seq"),
            P("dp", "seq"),
            P("seq"),
            P("dp", "seq"),
            P("dp", "seq"),
            P("seq", "dp"),
        ),
        out_specs=(
            P("dp", "seq", None),
            P("dp", "seq", None),
            P("seq"),
            P("dp", "seq"),
            P("seq"),
            P("dp", "seq"),
            P("seq"),
            P("dp", "seq"),
            P("seq"),
            P("dp", "seq"),
            P("seq"),
            P("dp", "seq"),
            P("dp", "seq"),
            P("seq", "dp"),
        ),
        check_vma=False,
    )
```

```python
import functools

import jax
import jax.numpy as jnp
from jax import lax
from jax.experimental import pallas as pl
from jax.experimental.pallas import tpu as pltpu
from jax.sharding import PartitionSpec as P

H = 14
KVH = 2
HD = 64


norm_eps = 1e-06
rope_base = 1000000.0


def contract(left_mat, right_mat, left_dim, right_dim):
    return lax.dot_general(
        left_mat,
        right_mat,
        (((left_dim,), (right_dim,)), ((), ())),
        preferred_element_type=jnp.float32,
    )


def angle_tables(positions, head_dim):
    half_dim = head_dim // 2
    frequency = rope_base ** (-2.0 * jnp.arange(half_dim, dtype=jnp.float32) / head_dim)
    angles = positions.astype(jnp.float32)[:, None] * frequency[None, :]
    return (jnp.cos(angles)[:, None, :], jnp.sin(angles)[:, None, :])


def rotate(heads_field, cosine, sine_table):
    half_dim = heads_field.shape[-1] // 2
    first_half = heads_field[..., :half_dim]
    second = heads_field[..., half_dim:]
    return jnp.concatenate(
        [first_half * cosine - second * sine_table, second * cosine + first_half * sine_table],
        axis=-1,
    )


def unrotate(grad_field, cosine, sine_table):
    half_dim = grad_field.shape[-1] // 2
    first_half = grad_field[..., :half_dim]
    second = grad_field[..., half_dim:]
    return jnp.concatenate(
        [first_half * cosine + second * sine_table, second * cosine - first_half * sine_table],
        axis=-1,
    )


def score_block(query_rot, key_all, query_seg, key_seg, query_pos, key_pos):
    scores = (
        jnp.einsum("qgjd,kgd->gjqk", query_rot, key_all, preferred_element_type=jnp.float32) * 0.125
    )
    allowed = (query_seg[:, None] == key_seg[None, :]) & (query_pos[:, None] >= key_pos[None, :])
    return jnp.where(allowed, scores, -1e30)


MESH = pl.DeviceIdType.MESH
VMEM_BYTES = 56 * 1024 * 1024


def places(seq_count, chip_count):
    d, s = lax.axis_index("dp"), lax.axis_index("seq")
    chip = lax.div(d, 2)
    core = d - 2 * chip
    sibling = (d + 1 - 2 * core, s)
    chips = [lax.rem(chip + k, chip_count) for k in range(chip_count)]
    seqs = [lax.rem(s + k, seq_count) for k in range(seq_count)]
    return d, s, chip, core, sibling, chips, seqs


def greet(partners):
    barrier = pltpu.get_barrier_semaphore()
    for partner in partners:
        pl.semaphore_signal(barrier, inc=1, device_id=partner, device_id_type=MESH)
    pl.semaphore_wait(barrier, len(partners))


def push(source, target, send_sem, recv_sem, device):
    copy = pltpu.make_async_remote_copy(
        src_ref=source,
        dst_ref=target,
        send_sem=send_sem,
        recv_sem=recv_sem,
        device_id=device,
        device_id_type=MESH,
    )
    copy.start()
    return copy


def gather_kernel(
    S, C, attn, vec, dy, gate, up, down,
    attn_all, vec_all, dy_all, gate_all, up_all, down_all,
    own_sem, s_send, s_recv, c_send, c_recv, p_send, p_recv,
):
    d, s, chip, core, sibling, chips, seqs = places(S, C)
    greet(
        [(d, seqs[k]) for k in range(1, S)]
        + [(2 * chips[k] + core, s) for k in range(1, C)]
        + [sibling]
    )
    seq_items = [(attn, attn_all.at[d, s]), (vec, vec_all.at[s]), (dy, dy_all.at[s])]
    seq_copies = []
    for i, (source, target) in enumerate(seq_items):
        seq_copies.append(
            [
                push(source, target, s_send.at[i, k], s_recv.at[i, k], (d, seqs[k]))
                for k in range(1, S)
            ]
        )
    dp_items = [(gate, gate_all), (up, up_all), (down, down_all)]
    own = []
    for i, (source, target) in enumerate(
        seq_items + [(source, whole.at[d]) for source, whole in dp_items]
    ):
        copy = pltpu.make_async_copy(source, target, own_sem.at[i])
        copy.start()
        own.append(copy)

    def spread(j, source, whole):
        far = [
            push(source, whole.at[d], c_send.at[j, k], c_recv.at[j, k], (2 * chips[k] + core, s))
            for k in range(1, C)
        ]
        near = push(source, whole.at[d], p_send.at[j, 0], p_recv.at[j, 0], sibling)
        return far, near

    copies = [spread(j, *item) for j, item in enumerate(dp_items)]
    own[0].wait()
    for copy in seq_copies[0]:
        copy.wait_recv()
    copies.append(spread(3, attn_all.at[d], attn_all))
    wholes = [gate_all, up_all, down_all, attn_all]
    near_copies = []
    for j in range(4):
        near_copies.append(copies[j][1])
        for k in range(1, C):
            copies[j][0][k - 1].wait_recv()
            slot = 2 * lax.rem(chip - k + C, C) + core
            block = wholes[j].at[slot]
            near_copies.append(push(block, block, p_send.at[j, k], p_recv.at[j, k], sibling))
    for copy in own[1:]:
        copy.wait()
    for copy in seq_copies[0]:
        copy.wait_send()
    for group in seq_copies[1:]:
        for copy in group:
            copy.wait()
    for far, _ in copies:
        for copy in far:
            copy.wait_send()
    for copy in near_copies:
        copy.wait()


def gather_all(S, DP, attn, vec, dy, gate, up, down):
    C = DP // 2

    def out(*shape):
        return jax.ShapeDtypeStruct(shape, jnp.bfloat16)

    dma = pltpu.SemaphoreType.DMA
    return pl.pallas_call(
        functools.partial(gather_kernel, S, C),
        out_shape=[
            out(DP, S, *attn.shape),
            out(S, *vec.shape),
            out(S, *dy.shape),
            out(DP, *gate.shape),
            out(DP, *up.shape),
            out(DP, *down.shape),
        ],
        in_specs=[pl.BlockSpec(memory_space=pl.ANY)] * 6,
        out_specs=[pl.BlockSpec(memory_space=pl.ANY)] * 6,
        scratch_shapes=[
            dma((6,)),
            dma((3, S)),
            dma((3, S)),
            dma((4, C)),
            dma((4, C)),
            dma((4, C)),
            dma((4, C)),
        ],
        compiler_params=pltpu.CompilerParams(
            collective_id=0, has_side_effects=True, vmem_limit_bytes=VMEM_BYTES
        ),
    )(attn, vec, dy, gate, up, down)


def scatter_kernel(
    S, C, attn, gate, up, down, small,
    o_attn, o_gate, o_up, o_down, o_small,
    attn_sib, gate_sib, up_sib, down_sib,
    attn_sum, gate_sum, up_sum, down_sum,
    attn_far, gate_far, up_far, down_far,
    seq_part, seq_far, small_seq, small_own, small_sib, small_chip,
    n_send, n_recv, c_send, c_recv, s_send, s_recv, m_send, m_recv,
):
    d, s, chip, core, sibling, chips, seqs = places(S, C)
    greet(
        [(d, seqs[k]) for k in range(1, S)]
        + [(2 * chips[k] + core, s) for k in range(1, C)]
        + [sibling]
    )
    items = [
        (attn, attn_sib, attn_sum, attn_far),
        (gate, gate_sib, gate_sum, gate_far),
        (up, up_sib, up_sum, up_far),
        (down, down_sib, down_sum, down_far),
    ]
    small_copies = [
        push(small.at[seqs[k]], small_seq.at[k - 1], m_send.at[0, k], m_recv.at[0, k], (d, seqs[k]))
        for k in range(1, S)
    ]
    order = list(range(1, C)) + [0]
    near = [
        {
            k: push(
                part.at[2 * chips[k] + 1 - core],
                sib.at[k],
                n_send.at[j, k],
                n_recv.at[j, k],
                sibling,
            )
            for k in order
        }
        for j, (part, sib, _, _) in enumerate(items)
    ]
    far = []
    for j, (part, sib, total, away) in enumerate(items):
        group = []
        for k in range(1, C):
            near[j][k].wait_recv()
            total[k - 1] = (
                part[2 * chips[k] + core].astype(jnp.float32) + sib[k].astype(jnp.float32)
            ).astype(jnp.bfloat16)
            group.append(
                push(
                    total.at[k - 1],
                    away.at[k - 1],
                    c_send.at[j, k],
                    c_recv.at[j, k],
                    (2 * chips[k] + core, s),
                )
            )
        far.append(group)

    for copy in small_copies:
        copy.wait()
    row_sum = small[s]
    for k in range(1, S):
        row_sum = row_sum + small_seq[k - 1]
    small_own[...] = row_sum
    pair = push(small_own, small_sib, m_send.at[1, 0], m_recv.at[1, 0], sibling)
    pair.wait()
    small_chip[chip] = small_own[...] + small_sib[...]
    chip_copies = [
        push(
            small_chip.at[chip],
            small_chip.at[chip],
            m_send.at[2, k],
            m_recv.at[2, k],
            (2 * chips[k] + core, s),
        )
        for k in range(1, C)
    ]

    def finish(j):
        part, sib, _, away = items[j]
        near[j][0].wait_recv()
        total = part[d].astype(jnp.float32) + sib[0].astype(jnp.float32)
        for k in range(1, C):
            far[j][k - 1].wait_recv()
            total = total + away[k - 1].astype(jnp.float32)
        return total

    seq_part[...] = finish(0).astype(jnp.bfloat16)
    seq_copies = [
        push(seq_part.at[seqs[k]], seq_far.at[k - 1], s_send.at[k], s_recv.at[k], (d, seqs[k]))
        for k in range(1, S)
    ]
    for j, out in ((1, o_gate), (2, o_up), (3, o_down)):
        out[...] = finish(j)
    for copy in chip_copies:
        copy.wait()
    total = small_chip[0]
    for k in range(1, C):
        total = total + small_chip[k]
    o_small[...] = total
    for copy in seq_copies:
        copy.wait()
    total = seq_part[s].astype(jnp.float32)
    for k in range(1, S):
        total = total + seq_far[k - 1].astype(jnp.float32)
    o_attn[...] = total
    for j in range(4):
        for k in range(C):
            near[j][k].wait_send()
        for copy in far[j]:
            copy.wait_send()


def scatter_all(S, DP, attn, gate, up, down, small):
    C = DP // 2
    blocks = [attn.shape[1:], gate.shape[1:], up.shape[1:], down.shape[1:]]

    def low(*shape):
        return pltpu.VMEM(shape, jnp.bfloat16)

    def wide(*shape):
        return pltpu.VMEM(shape, jnp.float32)

    def out(*shape):
        return jax.ShapeDtypeStruct(shape, jnp.float32)

    dma = pltpu.SemaphoreType.DMA
    return pl.pallas_call(
        functools.partial(scatter_kernel, S, C),
        out_shape=[
            out(*attn.shape[2:]),
            out(*blocks[1]),
            out(*blocks[2]),
            out(*blocks[3]),
            out(*small.shape[1:]),
        ],
        in_specs=[pl.BlockSpec(memory_space=pltpu.VMEM)] * 5,
        out_specs=[pl.BlockSpec(memory_space=pltpu.VMEM)] * 5,
        scratch_shapes=[low(C, *block) for block in blocks]
        + [low(C - 1, *block) for block in blocks]
        + [low(C - 1, *block) for block in blocks]
        + [
            low(S, *attn.shape[2:]),
            low(S - 1, *attn.shape[2:]),
            wide(S - 1, *small.shape[1:]),
            wide(*small.shape[1:]),
            wide(*small.shape[1:]),
            wide(C, *small.shape[1:]),
            dma((4, C)),
            dma((4, C)),
            dma((4, C)),
            dma((4, C)),
            dma((S,)),
            dma((S,)),
            dma((3, max(S, C))),
            dma((3, max(S, C))),
        ],
        compiler_params=pltpu.CompilerParams(
            collective_id=1, has_side_effects=True, vmem_limit_bytes=VMEM_BYTES
        ),
    )(attn, gate, up, down, small)


def on_device(
    tokens,
    segments,
    cotangent,
    attn_gain,
    w_query,
    b_query,
    w_key,
    b_key,
    w_value,
    b_value,
    w_out,
    mlp_gain,
    w_gate,
    w_up,
    w_down,
):
    local_len = tokens.shape[1]
    model_width = tokens.shape[2]
    seq_count = lax.axis_size("seq")
    dp_count = lax.axis_size("dp")
    seq_place = lax.axis_index("seq")
    full_len = local_len * seq_count
    group_size = H // KVH
    kv_width = KVH * HD
    rows = w_query.shape[0]
    q_cols = w_query.shape[1]
    k_cols = w_key.shape[1]
    pack_cols = 2 * q_cols + 2 * k_cols

    def as_row(vector):
        return jnp.pad(vector, (0, pack_cols - vector.shape[0]))[None]

    attn_own = jnp.concatenate([w_query, w_out, w_key, w_value], axis=1)
    vec_own = jnp.concatenate(
        [
            jnp.concatenate([attn_gain, b_query, b_key, b_value])[None],
            as_row(mlp_gain),
            as_row(segments[0].astype(jnp.bfloat16)),
            jnp.zeros((13, pack_cols), jnp.bfloat16),
        ],
        axis=0,
    )
    d_result = cotangent[0]
    attn_all, by_seq, d_result_all, mat_gate, mat_up, mat_down = gather_all(
        seq_count, dp_count, attn_own, vec_own, d_result, w_gate, w_up, w_down.T
    )
    d_result_all = d_result_all.reshape(full_len, model_width)
    mat_gate = mat_gate.reshape(model_width, -1)
    mat_up = mat_up.reshape(model_width, -1)
    mat_down = mat_down.reshape(model_width, -1)
    attn_all = attn_all.transpose(0, 2, 1, 3).reshape(model_width, seq_count, pack_cols)
    mat_query = attn_all[:, :, :q_cols].reshape(model_width, model_width)
    mat_out = attn_all[:, :, q_cols : 2 * q_cols].reshape(model_width, model_width)
    mat_key = attn_all[:, :, 2 * q_cols : 2 * q_cols + k_cols].reshape(model_width, kv_width)
    mat_value = attn_all[:, :, 2 * q_cols + k_cols :].reshape(model_width, kv_width)
    vectors = by_seq[:, 0].astype(jnp.float32)
    gain_one = vectors[:, :q_cols].reshape(model_width)
    bias_query = vectors[:, q_cols : 2 * q_cols].reshape(model_width)
    bias_key = vectors[:, 2 * q_cols : 2 * q_cols + k_cols].reshape(kv_width)
    bias_value = vectors[:, 2 * q_cols + k_cols :].reshape(kv_width)
    gain_two = by_seq[:, 1, :q_cols].astype(jnp.float32).reshape(model_width)
    seg_all = by_seq[:, 2, :local_len].reshape(full_len)
    seg_own = segments[0].astype(jnp.bfloat16)

    own_pos = seq_place * local_len + jnp.arange(local_len, dtype=jnp.int32)
    all_pos = jnp.arange(full_len, dtype=jnp.int32)
    cosine, sine_table = angle_tables(own_pos, HD)
    inputs = tokens[0].astype(jnp.float32)
    scale_one = lax.rsqrt(jnp.mean(inputs * inputs, axis=-1, keepdims=True) + norm_eps)
    normed = (inputs * scale_one * gain_one).astype(jnp.bfloat16)
    query_lin = jnp.dot(normed, mat_query, preferred_element_type=jnp.float32) + bias_query
    key_lin = jnp.dot(normed, mat_key, preferred_element_type=jnp.float32) + bias_key
    value_lin = jnp.dot(normed, mat_value, preferred_element_type=jnp.float32) + bias_value
    query_rot = rotate(query_lin.reshape(local_len, H, HD), cosine, sine_table).astype(
        jnp.bfloat16
    )
    query_rot = query_rot.reshape(local_len, KVH, group_size, HD)
    key_rot = rotate(key_lin.reshape(local_len, KVH, HD), cosine, sine_table).astype(jnp.bfloat16)
    value_loc = value_lin.astype(jnp.bfloat16)
    kv_loc = jnp.concatenate([key_rot.reshape(local_len, kv_width), value_loc], axis=1)
    kv_all = lax.all_gather(kv_loc, "seq", axis=0, tiled=True)
    key_all = kv_all[:, :kv_width].reshape(full_len, KVH, HD)
    value_all = kv_all[:, kv_width:].reshape(full_len, KVH, HD)
    masked = score_block(query_rot, key_all, seg_own, seg_all, own_pos, all_pos)
    highest = jnp.max(masked, axis=-1, keepdims=True)
    weights = jnp.exp(masked - highest)
    totals = jnp.sum(weights, axis=-1, keepdims=True)
    prob_low = (weights / totals).astype(jnp.bfloat16)
    log_total = highest + jnp.log(totals)
    mixed = jnp.einsum("gjqk,kgd->qgjd", prob_low, value_all, preferred_element_type=jnp.float32)
    mixed = mixed.astype(jnp.bfloat16).reshape(local_len, model_width)
    residual = inputs + jnp.dot(mixed, mat_out, preferred_element_type=jnp.float32)
    scale_two = lax.rsqrt(jnp.mean(residual * residual, axis=-1, keepdims=True) + norm_eps)
    normed_loc = (residual * scale_two * gain_two).astype(jnp.bfloat16)

    normed_two = lax.all_gather(normed_loc, "seq", axis=0, tiled=True)
    gate_lin = jnp.dot(normed_two, mat_gate, preferred_element_type=jnp.float32)
    up_lin = jnp.dot(normed_two, mat_up, preferred_element_type=jnp.float32)
    d_hidden = jnp.dot(d_result_all, mat_down, preferred_element_type=jnp.float32)
    sigmoid_gate = 1.0 / (1.0 + jnp.exp(-gate_lin))
    silu_gate = gate_lin * sigmoid_gate
    hidden = (silu_gate * up_lin).astype(jnp.bfloat16)
    d_gate = (
        d_hidden * up_lin * (sigmoid_gate + gate_lin * sigmoid_gate * (1.0 - sigmoid_gate))
    ).astype(jnp.bfloat16)
    d_up = (d_hidden * silu_gate).astype(jnp.bfloat16)
    d_norm_all = (contract(d_gate, mat_gate, 1, 1) + contract(d_up, mat_up, 1, 1)).astype(
        jnp.bfloat16
    )
    d_norm_part = lax.psum_scatter(d_norm_all, "seq", scatter_dimension=0, tiled=True).astype(
        jnp.float32
    )
    branch_all = contract(hidden, mat_down, 1, 1).astype(jnp.bfloat16)
    branch_all, d_norm_part = lax.optimization_barrier((branch_all, d_norm_part))
    branch_sum = lax.psum_scatter(branch_all, "seq", scatter_dimension=0, tiled=True)
    output = (residual + branch_sum.astype(jnp.float32)).astype(jnp.bfloat16)[None]
    part_gate, part_up, part_down = (
        contract(left, right, 0, 0).astype(jnp.bfloat16).reshape(dp_count, rows, -1)
        for left, right in ((normed_two, d_gate), (normed_two, d_up), (d_result_all, hidden))
    )

    grad_gain_two = jnp.sum(d_norm_part * residual * scale_two, axis=0)
    d_scaled_two = d_norm_part * gain_two
    d_residual = (
        d_result.astype(jnp.float32)
        + scale_two * d_scaled_two
        - residual * scale_two**3 * jnp.mean(d_scaled_two * residual, axis=-1, keepdims=True)
    )
    d_attn = d_residual.astype(jnp.bfloat16)
    grad_out = contract(mixed, d_attn, 0, 0)
    d_mixed = (
        contract(d_attn, mat_out, 1, 1)
        .astype(jnp.bfloat16)
        .reshape(local_len, KVH, group_size, HD)
    )
    masked = score_block(query_rot, key_all, seg_own, seg_all, own_pos, all_pos)
    prob_full = jnp.exp(masked - log_total)
    prob_low = prob_full.astype(jnp.bfloat16)
    d_probs = jnp.einsum("qgjd,kgd->gjqk", d_mixed, value_all, preferred_element_type=jnp.float32)
    d_value_full = jnp.einsum(
        "gjqk,qgjd->kgd", prob_low, d_mixed, preferred_element_type=jnp.float32
    )
    d_scores = (
        prob_full * (d_probs - jnp.sum(d_probs * prob_full, axis=-1, keepdims=True))
    ).astype(jnp.bfloat16)
    d_key_full = (
        jnp.einsum("gjqk,qgjd->kgd", d_scores, query_rot, preferred_element_type=jnp.float32)
        * 0.125
    )
    d_kv_full = jnp.concatenate(
        [d_key_full.reshape(full_len, kv_width), d_value_full.reshape(full_len, kv_width)], axis=1
    ).astype(jnp.bfloat16)
    d_kv_loc = lax.psum_scatter(d_kv_full, "seq", scatter_dimension=0, tiled=True)
    d_query_rot = (
        jnp.einsum("gjqk,kgd->qgjd", d_scores, key_all, preferred_element_type=jnp.float32) * 0.125
    ).reshape(local_len, H, HD)
    d_query_lin = (
        unrotate(d_query_rot, cosine, sine_table)
        .astype(jnp.bfloat16)
        .reshape(local_len, model_width)
    )
    d_key_loc = d_kv_loc[:, :kv_width].astype(jnp.float32).reshape(local_len, KVH, HD)
    d_key_lin = (
        unrotate(d_key_loc, cosine, sine_table).astype(jnp.bfloat16).reshape(local_len, kv_width)
    )
    d_value_lin = d_kv_loc[:, kv_width:]
    grad_query = contract(normed, d_query_lin, 0, 0)
    grad_key = contract(normed, d_key_lin, 0, 0)
    grad_value = contract(normed, d_value_lin, 0, 0)

    attn_grads = jnp.concatenate(
        [
            item.astype(jnp.bfloat16).reshape(dp_count, rows, seq_count, -1)
            for item in (grad_query, grad_out, grad_key, grad_value)
        ],
        axis=3,
    ).transpose(0, 2, 1, 3)
    grad_bias_query = jnp.sum(d_query_lin, axis=0, dtype=jnp.float32)
    grad_bias_key = jnp.sum(d_key_lin, axis=0, dtype=jnp.float32)
    grad_bias_value = jnp.sum(d_value_lin, axis=0, dtype=jnp.float32)
    d_normed = (
        contract(d_query_lin, mat_query, 1, 1)
        + contract(d_key_lin, mat_key, 1, 1)
        + contract(d_value_lin, mat_value, 1, 1)
    )
    grad_gain_one = jnp.sum(d_normed * inputs * scale_one, axis=0)
    d_scaled = d_normed * gain_one
    d_inputs = (
        d_residual
        + scale_one * d_scaled
        - inputs * scale_one**3 * jnp.mean(d_scaled * inputs, axis=-1, keepdims=True)
    )
    small = jnp.concatenate(
        [
            item.reshape(seq_count, -1)
            for item in (
                grad_gain_one,
                grad_bias_query,
                grad_gain_two,
                grad_bias_key,
                grad_bias_value,
            )
        ],
        axis=1,
    )
    small = jnp.pad(small[:, None], ((0, 0), (0, 7), (0, -small.shape[1] % 128)))
    attn_grads, grad_gate, grad_up, grad_down, small = scatter_all(
        seq_count, dp_count, attn_grads, part_gate, part_up, part_down, small
    )
    small = small[0]
    return (
        output,
        d_inputs[None],
        small[:q_cols],
        attn_grads[:, :q_cols],
        small[q_cols : 2 * q_cols],
        attn_grads[:, 2 * q_cols : 2 * q_cols + k_cols],
        small[3 * q_cols : 3 * q_cols + k_cols],
        attn_grads[:, 2 * q_cols + k_cols :],
        small[3 * q_cols + k_cols : 3 * q_cols + 2 * k_cols],
        attn_grads[:, q_cols : 2 * q_cols],
        small[2 * q_cols : 3 * q_cols],
        grad_gate,
        grad_up,
        grad_down.T,
    )


def solution(mesh):
    return jax.shard_map(
        on_device,
        mesh=mesh,
        in_specs=(
            P("dp", "seq", None),
            P("dp", "seq"),
            P("dp", "seq", None),
            P("seq"),
            P("dp", "seq"),
            P("seq"),
            P("dp", "seq"),
            P("seq"),
            P("dp", "seq"),
            P("seq"),
            P("dp", "seq"),
            P("seq"),
            P("dp", "seq"),
            P("dp", "seq"),
            P("seq", "dp"),
        ),
        out_specs=(
            P("dp", "seq", None),
            P("dp", "seq", None),
            P("seq"),
            P("dp", "seq"),
            P("seq"),
            P("dp", "seq"),
            P("seq"),
            P("dp", "seq"),
            P("seq"),
            P("dp", "seq"),
            P("seq"),
            P("dp", "seq"),
            P("dp", "seq"),
            P("seq", "dp"),
        ),
        check_vma=False,
    )
```

```python
import functools

import jax
import jax.numpy as jnp
from jax import lax
from jax.experimental import pallas as pl
from jax.experimental.pallas import tpu as pltpu
from jax.sharding import PartitionSpec as P

H = 14
KVH = 2
HD = 64


norm_eps = 1e-06
rope_base = 1000000.0


def contract(left_mat, right_mat, left_dim, right_dim):
    return lax.dot_general(
        left_mat,
        right_mat,
        (((left_dim,), (right_dim,)), ((), ())),
        preferred_element_type=jnp.float32,
    )


def angle_tables(positions, head_dim):
    half_dim = head_dim // 2
    frequency = rope_base ** (-2.0 * jnp.arange(half_dim, dtype=jnp.float32) / head_dim)
    angles = positions.astype(jnp.float32)[:, None] * frequency[None, :]
    return (jnp.cos(angles)[:, None, :], jnp.sin(angles)[:, None, :])


def rotate(heads_field, cosine, sine_table):
    half_dim = heads_field.shape[-1] // 2
    first_half = heads_field[..., :half_dim]
    second = heads_field[..., half_dim:]
    return jnp.concatenate(
        [first_half * cosine - second * sine_table, second * cosine + first_half * sine_table],
        axis=-1,
    )


def unrotate(grad_field, cosine, sine_table):
    half_dim = grad_field.shape[-1] // 2
    first_half = grad_field[..., :half_dim]
    second = grad_field[..., half_dim:]
    return jnp.concatenate(
        [first_half * cosine + second * sine_table, second * cosine - first_half * sine_table],
        axis=-1,
    )


def score_block(query_rot, key_all, query_seg, key_seg, query_pos, key_pos):
    scores = (
        jnp.einsum("qgjd,kgd->gjqk", query_rot, key_all, preferred_element_type=jnp.float32) * 0.125
    )
    allowed = (query_seg[:, None] == key_seg[None, :]) & (query_pos[:, None] >= key_pos[None, :])
    return jnp.where(allowed, scores, -1e30)


MESH = pl.DeviceIdType.MESH
VMEM_BYTES = 56 * 1024 * 1024


def places(seq_count, chip_count):
    d, s = lax.axis_index("dp"), lax.axis_index("seq")
    chip = lax.div(d, 2)
    core = d - 2 * chip
    sibling = (d + 1 - 2 * core, s)
    chips = [lax.rem(chip + k, chip_count) for k in range(chip_count)]
    seqs = [lax.rem(s + k, seq_count) for k in range(seq_count)]
    return d, s, chip, core, sibling, chips, seqs


def greet(partners):
    barrier = pltpu.get_barrier_semaphore()
    for partner in partners:
        pl.semaphore_signal(barrier, inc=1, device_id=partner, device_id_type=MESH)
    pl.semaphore_wait(barrier, len(partners))


def push(source, target, send_sem, recv_sem, device):
    copy = pltpu.make_async_remote_copy(
        src_ref=source,
        dst_ref=target,
        send_sem=send_sem,
        recv_sem=recv_sem,
        device_id=device,
        device_id_type=MESH,
    )
    copy.start()
    return copy


def gather_kernel(
    S, C, attn, vec, dy, gate, up, down,
    attn_all, vec_all, dy_all, gate_all, up_all, down_all,
    own_sem, s_send, s_recv, c_send, c_recv, p_send, p_recv,
):
    d, s, chip, core, sibling, chips, seqs = places(S, C)
    greet(
        [(d, seqs[k]) for k in range(1, S)]
        + [(2 * chips[k] + core, s) for k in range(1, C)]
        + [sibling]
    )
    seq_items = [(attn, attn_all.at[d, s]), (vec, vec_all.at[s]), (dy, dy_all.at[s])]
    seq_copies = []
    for i, (source, target) in enumerate(seq_items):
        seq_copies.append(
            [
                push(source, target, s_send.at[i, k], s_recv.at[i, k], (d, seqs[k]))
                for k in range(1, S)
            ]
        )
    dp_items = [(gate, gate_all), (up, up_all), (down, down_all)]
    own = []
    for i, (source, target) in enumerate(
        seq_items + [(source, whole.at[d]) for source, whole in dp_items]
    ):
        copy = pltpu.make_async_copy(source, target, own_sem.at[i])
        copy.start()
        own.append(copy)

    def spread(j, source, whole):
        far = [
            push(source, whole.at[d], c_send.at[j, k], c_recv.at[j, k], (2 * chips[k] + core, s))
            for k in range(1, C)
        ]
        near = push(source, whole.at[d], p_send.at[j, 0], p_recv.at[j, 0], sibling)
        return far, near

    copies = [spread(j, *item) for j, item in enumerate(dp_items)]
    own[0].wait()
    for copy in seq_copies[0]:
        copy.wait_recv()
    copies.append(spread(3, attn_all.at[d], attn_all))
    wholes = [gate_all, up_all, down_all, attn_all]
    near_copies = []
    for j in range(4):
        near_copies.append(copies[j][1])
        for k in range(1, C):
            copies[j][0][k - 1].wait_recv()
            slot = 2 * lax.rem(chip - k + C, C) + core
            block = wholes[j].at[slot]
            near_copies.append(push(block, block, p_send.at[j, k], p_recv.at[j, k], sibling))
    for copy in own[1:]:
        copy.wait()
    for copy in seq_copies[0]:
        copy.wait_send()
    for group in seq_copies[1:]:
        for copy in group:
            copy.wait()
    for far, _ in copies:
        for copy in far:
            copy.wait_send()
    for copy in near_copies:
        copy.wait()


def gather_all(S, DP, attn, vec, dy, gate, up, down):
    C = DP // 2

    def out(*shape):
        return jax.ShapeDtypeStruct(shape, jnp.bfloat16)

    dma = pltpu.SemaphoreType.DMA
    return pl.pallas_call(
        functools.partial(gather_kernel, S, C),
        out_shape=[
            out(DP, S, *attn.shape),
            out(S, *vec.shape),
            out(S, *dy.shape),
            out(DP, *gate.shape),
            out(DP, *up.shape),
            out(DP, *down.shape),
        ],
        in_specs=[pl.BlockSpec(memory_space=pl.ANY)] * 6,
        out_specs=[pl.BlockSpec(memory_space=pl.ANY)] * 6,
        scratch_shapes=[
            dma((6,)),
            dma((3, S)),
            dma((3, S)),
            dma((4, C)),
            dma((4, C)),
            dma((4, C)),
            dma((4, C)),
        ],
        compiler_params=pltpu.CompilerParams(
            collective_id=0, has_side_effects=True, vmem_limit_bytes=VMEM_BYTES
        ),
    )(attn, vec, dy, gate, up, down)


def scatter_kernel(
    S, C, attn, gate, up, down, small,
    o_attn, o_gate, o_up, o_down, o_small,
    attn_sib, gate_sib, up_sib, down_sib,
    attn_sum, gate_sum, up_sum, down_sum,
    attn_far, gate_far, up_far, down_far,
    seq_part, seq_far, small_seq, small_own, small_sib, small_chip,
    n_send, n_recv, c_send, c_recv, s_send, s_recv, m_send, m_recv,
):
    d, s, chip, core, sibling, chips, seqs = places(S, C)
    greet(
        [(d, seqs[k]) for k in range(1, S)]
        + [(2 * chips[k] + core, s) for k in range(1, C)]
        + [sibling]
    )
    items = [
        (attn, attn_sib, attn_sum, attn_far),
        (gate, gate_sib, gate_sum, gate_far),
        (up, up_sib, up_sum, up_far),
        (down, down_sib, down_sum, down_far),
    ]
    small_copies = [
        push(small.at[seqs[k]], small_seq.at[k - 1], m_send.at[0, k], m_recv.at[0, k], (d, seqs[k]))
        for k in range(1, S)
    ]
    order = list(range(1, C)) + [0]
    near = [
        {
            k: push(
                part.at[2 * chips[k] + 1 - core],
                sib.at[k],
                n_send.at[j, k],
                n_recv.at[j, k],
                sibling,
            )
            for k in order
        }
        for j, (part, sib, _, _) in enumerate(items)
    ]
    far = []
    for j, (part, sib, total, away) in enumerate(items):
        group = []
        for k in range(1, C):
            near[j][k].wait_recv()
            total[k - 1] = (
                part[2 * chips[k] + core].astype(jnp.float32) + sib[k].astype(jnp.float32)
            ).astype(jnp.bfloat16)
            group.append(
                push(
                    total.at[k - 1],
                    away.at[k - 1],
                    c_send.at[j, k],
                    c_recv.at[j, k],
                    (2 * chips[k] + core, s),
                )
            )
        far.append(group)

    for copy in small_copies:
        copy.wait()
    row_sum = small[s]
    for k in range(1, S):
        row_sum = row_sum + small_seq[k - 1]
    small_own[...] = row_sum
    pair = push(small_own, small_sib, m_send.at[1, 0], m_recv.at[1, 0], sibling)
    pair.wait()
    small_chip[chip] = small_own[...] + small_sib[...]
    chip_copies = [
        push(
            small_chip.at[chip],
            small_chip.at[chip],
            m_send.at[2, k],
            m_recv.at[2, k],
            (2 * chips[k] + core, s),
        )
        for k in range(1, C)
    ]

    def finish(j):
        part, sib, _, away = items[j]
        near[j][0].wait_recv()
        total = part[d].astype(jnp.float32) + sib[0].astype(jnp.float32)
        for k in range(1, C):
            far[j][k - 1].wait_recv()
            total = total + away[k - 1].astype(jnp.float32)
        return total

    seq_part[...] = finish(0).astype(jnp.bfloat16)
    seq_copies = [
        push(seq_part.at[seqs[k]], seq_far.at[k - 1], s_send.at[k], s_recv.at[k], (d, seqs[k]))
        for k in range(1, S)
    ]
    for j, out in ((1, o_gate), (2, o_up), (3, o_down)):
        out[...] = finish(j)
    for copy in chip_copies:
        copy.wait()
    total = small_chip[0]
    for k in range(1, C):
        total = total + small_chip[k]
    o_small[...] = total
    for copy in seq_copies:
        copy.wait()
    total = seq_part[s].astype(jnp.float32)
    for k in range(1, S):
        total = total + seq_far[k - 1].astype(jnp.float32)
    o_attn[...] = total
    for j in range(4):
        for k in range(C):
            near[j][k].wait_send()
        for copy in far[j]:
            copy.wait_send()


def scatter_all(S, DP, attn, gate, up, down, small):
    C = DP // 2
    blocks = [attn.shape[1:], gate.shape[1:], up.shape[1:], down.shape[1:]]

    def low(*shape):
        return pltpu.VMEM(shape, jnp.bfloat16)

    def wide(*shape):
        return pltpu.VMEM(shape, jnp.float32)

    def out(*shape):
        return jax.ShapeDtypeStruct(shape, jnp.float32)

    dma = pltpu.SemaphoreType.DMA
    return pl.pallas_call(
        functools.partial(scatter_kernel, S, C),
        out_shape=[
            out(*attn.shape[2:]),
            out(*blocks[1]),
            out(*blocks[2]),
            out(*blocks[3]),
            out(*small.shape[1:]),
        ],
        in_specs=[pl.BlockSpec(memory_space=pltpu.VMEM)] * 5,
        out_specs=[pl.BlockSpec(memory_space=pltpu.VMEM)] * 5,
        scratch_shapes=[low(C, *block) for block in blocks]
        + [low(C - 1, *block) for block in blocks]
        + [low(C - 1, *block) for block in blocks]
        + [
            low(S, *attn.shape[2:]),
            low(S - 1, *attn.shape[2:]),
            wide(S - 1, *small.shape[1:]),
            wide(*small.shape[1:]),
            wide(*small.shape[1:]),
            wide(C, *small.shape[1:]),
            dma((4, C)),
            dma((4, C)),
            dma((4, C)),
            dma((4, C)),
            dma((S,)),
            dma((S,)),
            dma((3, max(S, C))),
            dma((3, max(S, C))),
        ],
        compiler_params=pltpu.CompilerParams(
            collective_id=1, has_side_effects=True, vmem_limit_bytes=VMEM_BYTES
        ),
    )(attn, gate, up, down, small)


def on_device(
    tokens,
    segments,
    cotangent,
    attn_gain,
    w_query,
    b_query,
    w_key,
    b_key,
    w_value,
    b_value,
    w_out,
    mlp_gain,
    w_gate,
    w_up,
    w_down,
):
    local_len = tokens.shape[1]
    model_width = tokens.shape[2]
    seq_count = lax.axis_size("seq")
    dp_count = lax.axis_size("dp")
    seq_place = lax.axis_index("seq")
    full_len = local_len * seq_count
    group_size = H // KVH
    kv_width = KVH * HD
    rows = w_query.shape[0]
    q_cols = w_query.shape[1]
    k_cols = w_key.shape[1]
    pack_cols = 2 * q_cols + 2 * k_cols

    def as_row(vector):
        return jnp.pad(vector, (0, pack_cols - vector.shape[0]))[None]

    attn_own = jnp.concatenate([w_query, w_out, w_key, w_value], axis=1)
    vec_own = jnp.concatenate(
        [
            jnp.concatenate([attn_gain, b_query, b_key, b_value])[None],
            as_row(mlp_gain),
            as_row(segments[0].astype(jnp.bfloat16)),
            jnp.zeros((13, pack_cols), jnp.bfloat16),
        ],
        axis=0,
    )
    d_result = cotangent[0]
    attn_all, by_seq, d_result_all, mat_gate, mat_up, mat_down = gather_all(
        seq_count, dp_count, attn_own, vec_own, d_result, w_gate, w_up, w_down.T
    )
    d_result_all = d_result_all.reshape(full_len, model_width)
    mat_gate = mat_gate.reshape(model_width, -1)
    mat_up = mat_up.reshape(model_width, -1)
    mat_down = mat_down.reshape(model_width, -1)
    mat_attn = attn_all.transpose(0, 2, 1, 3).reshape(model_width, seq_count * pack_cols)

    def take(field, start, size):
        field = field.reshape(field.shape[0], seq_count, pack_cols)
        return field[:, :, start : start + size].reshape(field.shape[0], -1)

    def lay(query=None, out=None, key=None, value=None):
        def block(item, size):
            if item is None:
                return jnp.zeros((local_len, seq_count, size), jnp.bfloat16)
            return item.reshape(local_len, seq_count, size)

        return jnp.concatenate(
            [block(query, q_cols), block(out, q_cols), block(key, k_cols), block(value, k_cols)],
            axis=2,
        ).reshape(local_len, seq_count * pack_cols)

    vectors = by_seq[:, 0].astype(jnp.float32)
    gain_one = vectors[:, :q_cols].reshape(model_width)
    bias_query = vectors[:, q_cols : 2 * q_cols].reshape(model_width)
    bias_key = vectors[:, 2 * q_cols : 2 * q_cols + k_cols].reshape(kv_width)
    bias_value = vectors[:, 2 * q_cols + k_cols :].reshape(kv_width)
    gain_two = by_seq[:, 1, :q_cols].astype(jnp.float32).reshape(model_width)
    seg_all = by_seq[:, 2, :local_len].reshape(full_len)
    seg_own = segments[0].astype(jnp.bfloat16)

    own_pos = seq_place * local_len + jnp.arange(local_len, dtype=jnp.int32)
    all_pos = jnp.arange(full_len, dtype=jnp.int32)
    cosine, sine_table = angle_tables(own_pos, HD)
    inputs = tokens[0].astype(jnp.float32)
    scale_one = lax.rsqrt(jnp.mean(inputs * inputs, axis=-1, keepdims=True) + norm_eps)
    normed = (inputs * scale_one * gain_one).astype(jnp.bfloat16)
    lin = jnp.dot(normed, mat_attn, preferred_element_type=jnp.float32)
    query_lin = take(lin, 0, q_cols) + bias_query
    key_lin = take(lin, 2 * q_cols, k_cols) + bias_key
    value_lin = take(lin, 2 * q_cols + k_cols, k_cols) + bias_value
    query_rot = rotate(query_lin.reshape(local_len, H, HD), cosine, sine_table).astype(
        jnp.bfloat16
    )
    query_rot = query_rot.reshape(local_len, KVH, group_size, HD)
    key_rot = rotate(key_lin.reshape(local_len, KVH, HD), cosine, sine_table).astype(jnp.bfloat16)
    value_loc = value_lin.astype(jnp.bfloat16)
    kv_loc = jnp.concatenate([key_rot.reshape(local_len, kv_width), value_loc], axis=1)
    kv_all = lax.all_gather(kv_loc, "seq", axis=0, tiled=True)
    key_all = kv_all[:, :kv_width].reshape(full_len, KVH, HD)
    value_all = kv_all[:, kv_width:].reshape(full_len, KVH, HD)
    masked = score_block(query_rot, key_all, seg_own, seg_all, own_pos, all_pos)
    highest = jnp.max(masked, axis=-1, keepdims=True)
    weights = jnp.exp(masked - highest)
    totals = jnp.sum(weights, axis=-1, keepdims=True)
    prob_low = (weights / totals).astype(jnp.bfloat16)
    log_total = highest + jnp.log(totals)
    mixed = jnp.einsum("gjqk,kgd->qgjd", prob_low, value_all, preferred_element_type=jnp.float32)
    mixed = mixed.astype(jnp.bfloat16).reshape(local_len, model_width)
    residual = inputs + take(
        jnp.dot(mixed, mat_attn, preferred_element_type=jnp.float32), q_cols, q_cols
    )
    scale_two = lax.rsqrt(jnp.mean(residual * residual, axis=-1, keepdims=True) + norm_eps)
    normed_loc = (residual * scale_two * gain_two).astype(jnp.bfloat16)

    normed_two = lax.all_gather(normed_loc, "seq", axis=0, tiled=True)
    gate_lin = jnp.dot(normed_two, mat_gate, preferred_element_type=jnp.float32)
    up_lin = jnp.dot(normed_two, mat_up, preferred_element_type=jnp.float32)
    d_hidden = jnp.dot(d_result_all, mat_down, preferred_element_type=jnp.float32)
    sigmoid_gate = 1.0 / (1.0 + jnp.exp(-gate_lin))
    silu_gate = gate_lin * sigmoid_gate
    hidden = (silu_gate * up_lin).astype(jnp.bfloat16)
    d_gate = (
        d_hidden * up_lin * (sigmoid_gate + gate_lin * sigmoid_gate * (1.0 - sigmoid_gate))
    ).astype(jnp.bfloat16)
    d_up = (d_hidden * silu_gate).astype(jnp.bfloat16)
    d_norm_all = (contract(d_gate, mat_gate, 1, 1) + contract(d_up, mat_up, 1, 1)).astype(
        jnp.bfloat16
    )
    d_norm_part = lax.psum_scatter(d_norm_all, "seq", scatter_dimension=0, tiled=True)
    branch_all = contract(hidden, mat_down, 1, 1).astype(jnp.bfloat16)
    part_gate, part_up, part_down = (
        contract(left, right, 0, 0).astype(jnp.bfloat16).reshape(dp_count, rows, -1)
        for left, right in ((normed_two, d_gate), (normed_two, d_up), (d_result_all, hidden))
    )

    d_norm_part, branch_all, part_gate, part_up, part_down = lax.optimization_barrier(
        (d_norm_part, branch_all, part_gate, part_up, part_down)
    )
    d_norm_part = d_norm_part.astype(jnp.float32)
    branch_sum = lax.psum_scatter(branch_all, "seq", scatter_dimension=0, tiled=True)
    output = (residual + branch_sum.astype(jnp.float32)).astype(jnp.bfloat16)[None]

    grad_gain_two = jnp.sum(d_norm_part * residual * scale_two, axis=0)
    d_scaled_two = d_norm_part * gain_two
    d_residual = (
        d_result.astype(jnp.float32)
        + scale_two * d_scaled_two
        - residual * scale_two**3 * jnp.mean(d_scaled_two * residual, axis=-1, keepdims=True)
    )
    d_attn = d_residual.astype(jnp.bfloat16)
    d_attn_laid = lay(out=d_attn)
    d_mixed = (
        contract(d_attn_laid, mat_attn, 1, 1)
        .astype(jnp.bfloat16)
        .reshape(local_len, KVH, group_size, HD)
    )
    masked = score_block(query_rot, key_all, seg_own, seg_all, own_pos, all_pos)
    prob_full = jnp.exp(masked - log_total)
    prob_low = prob_full.astype(jnp.bfloat16)
    d_probs = jnp.einsum("qgjd,kgd->gjqk", d_mixed, value_all, preferred_element_type=jnp.float32)
    d_value_full = jnp.einsum(
        "gjqk,qgjd->kgd", prob_low, d_mixed, preferred_element_type=jnp.float32
    )
    d_scores = (
        prob_full * (d_probs - jnp.sum(d_probs * prob_full, axis=-1, keepdims=True))
    ).astype(jnp.bfloat16)
    d_key_full = (
        jnp.einsum("gjqk,qgjd->kgd", d_scores, query_rot, preferred_element_type=jnp.float32)
        * 0.125
    )
    d_kv_full = jnp.concatenate(
        [d_key_full.reshape(full_len, kv_width), d_value_full.reshape(full_len, kv_width)], axis=1
    ).astype(jnp.bfloat16)
    d_kv_loc = lax.psum_scatter(d_kv_full, "seq", scatter_dimension=0, tiled=True)
    d_query_rot = (
        jnp.einsum("gjqk,kgd->qgjd", d_scores, key_all, preferred_element_type=jnp.float32) * 0.125
    ).reshape(local_len, H, HD)
    d_query_lin = (
        unrotate(d_query_rot, cosine, sine_table)
        .astype(jnp.bfloat16)
        .reshape(local_len, model_width)
    )
    d_key_loc = d_kv_loc[:, :kv_width].astype(jnp.float32).reshape(local_len, KVH, HD)
    d_key_lin = (
        unrotate(d_key_loc, cosine, sine_table).astype(jnp.bfloat16).reshape(local_len, kv_width)
    )
    d_value_lin = d_kv_loc[:, kv_width:]
    d_lin_laid = lay(query=d_query_lin, key=d_key_lin, value=d_value_lin)

    attn_grads = contract(
        jnp.concatenate([normed, mixed], axis=0),
        jnp.concatenate([d_lin_laid, d_attn_laid], axis=0),
        0,
        0,
    )
    attn_grads = attn_grads.astype(jnp.bfloat16).reshape(dp_count, rows, seq_count, pack_cols)
    attn_grads = attn_grads.transpose(0, 2, 1, 3)

    grad_bias_query = jnp.sum(d_query_lin, axis=0, dtype=jnp.float32)
    grad_bias_key = jnp.sum(d_key_lin, axis=0, dtype=jnp.float32)
    grad_bias_value = jnp.sum(d_value_lin, axis=0, dtype=jnp.float32)
    d_normed = contract(d_lin_laid, mat_attn, 1, 1)
    grad_gain_one = jnp.sum(d_normed * inputs * scale_one, axis=0)
    d_scaled = d_normed * gain_one
    d_inputs = (
        d_residual
        + scale_one * d_scaled
        - inputs * scale_one**3 * jnp.mean(d_scaled * inputs, axis=-1, keepdims=True)
    )
    small = jnp.concatenate(
        [
            item.reshape(seq_count, -1)
            for item in (
                grad_gain_one,
                grad_bias_query,
                grad_gain_two,
                grad_bias_key,
                grad_bias_value,
            )
        ],
        axis=1,
    )
    small = jnp.pad(small[:, None], ((0, 0), (0, 7), (0, -small.shape[1] % 128)))
    attn_grads, grad_gate, grad_up, grad_down, small = scatter_all(
        seq_count, dp_count, attn_grads, part_gate, part_up, part_down, small
    )
    small = small[0]
    return (
        output,
        d_inputs[None],
        small[:q_cols],
        attn_grads[:, :q_cols],
        small[q_cols : 2 * q_cols],
        attn_grads[:, 2 * q_cols : 2 * q_cols + k_cols],
        small[3 * q_cols : 3 * q_cols + k_cols],
        attn_grads[:, 2 * q_cols + k_cols :],
        small[3 * q_cols + k_cols : 3 * q_cols + 2 * k_cols],
        attn_grads[:, q_cols : 2 * q_cols],
        small[2 * q_cols : 3 * q_cols],
        grad_gate,
        grad_up,
        grad_down.T,
    )


def solution(mesh):
    return jax.shard_map(
        on_device,
        mesh=mesh,
        in_specs=(
            P("dp", "seq", None),
            P("dp", "seq"),
            P("dp", "seq", None),
            P("seq"),
            P("dp", "seq"),
            P("seq"),
            P("dp", "seq"),
            P("seq"),
            P("dp", "seq"),
            P("seq"),
            P("dp", "seq"),
            P("seq"),
            P("dp", "seq"),
            P("dp", "seq"),
            P("seq", "dp"),
        ),
        out_specs=(
            P("dp", "seq", None),
            P("dp", "seq", None),
            P("seq"),
            P("dp", "seq"),
            P("seq"),
            P("dp", "seq"),
            P("seq"),
            P("dp", "seq"),
            P("seq"),
            P("dp", "seq"),
            P("seq"),
            P("dp", "seq"),
            P("dp", "seq"),
            P("seq", "dp"),
        ),
        check_vma=False,
    )
```
